32 devices in a mesh: groups: 2 (over x), row: 2 (over core), col: 8 (over z, y).
Axes of the slice: x: 2, y: 2, z: 4, core: 2. Of those that a mesh axis runs over, the one named last changes fastest.
Arguments:
- context: bfloat16 [2048, 12288], P('groups', ('row', 'col')), parts along dimension 0, may hold values from -6 to 6
- out_grad: bfloat16 [2048, 12288], P(('groups', 'row'), 'col'), parts along dimension 0, may hold values from -4 to 4
- weight: bfloat16 [12288, 12288], P('row', 'col'), may hold values from -0.078125 to 0.078125
Outputs:
- input_grad: bfloat16 [2048, 12288], P('groups', ('row', 'col')), parts along dimension 0
- weight_grad: bfloat16 [24576, 12288], P(('groups', 'row'), 'col'), parts along dimension 0
The draws below stay inside these ranges and needn't reach their ends.
There are 2 independent parts, one for each index of `groups`. The reference program is written for one: setup_inputs(seed, part) draws one part's arguments, and reference() takes and returns one part's arrays. A program takes and returns all parts, laid end to end along the dimension named above; an argument that names none is the same for every part. Nothing has to cross between parts.
All inputs are finite; a program needn't handle non-finite values.
Results may differ from the reference program's by a relative error of at most 0.012.
Values may be sent and summed in bfloat16 or wider, within the bound.
No kernel may reach another device: no remote copies, remote signals or barrier semaphores. Data moves between devices by JAX's collectives and lax.ppermute only.
A program may use at most 192 MiB of HBM per device.

```python
import jax
import jax.numpy as jnp
from jax import lax

D = 12288
TOKENS = 1024
N_COL = 8


def with_spikes(values, own_key, source, target, blocks, factor):
    def block_of(dim):
        return (jnp.arange(values.shape[dim]) // (values.shape[dim] // blocks)).reshape((-1,) + (1,) * (values.ndim - 1 - dim))

    near = jax.random.permutation(own_key, blocks)[block_of(target)]
    far = (block_of(target) + blocks // 2) % blocks
    return jnp.where((block_of(source) == near) | (block_of(source) == far), factor * values, values)


def steps_of(stream_key, dims, shards, least, largest):
    level, own = 1.0, jax.random.fold_in(stream_key, 6)
    for position, blocks in shards:
        draws = jnp.exp(jax.random.uniform(jax.random.fold_in(own, position), (blocks,), jnp.float32, least / len(shards), largest / len(shards)))
        level = level * jnp.repeat(draws, dims[position] // blocks).reshape([-1 if axis == position else 1 for axis in range(len(dims))])
    return level


def bell_draw(key, shape, deviation, reach, pieces=(), kind=jnp.bfloat16):
    level = steps_of(key, shape, pieces, -0.22, 0.18) if pieces else 1.0
    drawn = jax.random.normal(key, shape, jnp.float32) * deviation * level
    return jnp.minimum(jnp.maximum(drawn, -reach), reach).astype(kind)


def bell_draw_with(own_key, dims, scale, bound, shards, heavy, kind=jnp.bfloat16):
    entries = scale * jax.random.normal(own_key, dims, jnp.float32)
    if shards:
        entries = entries * steps_of(own_key, dims, shards, -0.22, 0.18)
    return jnp.clip(with_spikes(entries, jax.random.fold_in(own_key, 3), *heavy), -bound, bound).astype(kind)


def setup_inputs(seed: int = 0, part: int = 0) -> dict:
    keys = jax.random.split(jax.random.key(seed), 4)
    part_splits = jax.random.split(jax.random.fold_in(keys[3], part), 4)
    return {
        "context": bell_draw(part_splits[0], (TOKENS, D), 1.0, 6.0, ((1, 16),)),
        "out_grad": bell_draw(part_splits[1], (TOKENS, D), 0.25, 4.0, ((0, 2), (1, 8))),
        "weight": bell_draw_with(keys[2], (D, D), D ** -0.5, 0.078125, ((0, 2), (1, 8)), (1, 0, 8, 2.0)),
    }


def reference(context, out_grad, weight):
    blocks = N_COL
    width = D // blocks

    def step(total, index):
        start = (index * width).astype(jnp.int32)
        grad_block = lax.dynamic_slice_in_dim(out_grad, start, width, 1)
        weight_block = lax.dynamic_slice_in_dim(weight, start, width, 1)
        partial_block = jnp.dot(grad_block, weight_block.T, preferred_element_type=jnp.float32).astype(jnp.bfloat16)
        partial_block = lax.optimization_barrier(partial_block)
        return total + partial_block.astype(jnp.float32), None

    start_total = jnp.zeros((TOKENS, D), jnp.float32)
    total, _ = lax.scan(step, start_total, jnp.arange(blocks, dtype=jnp.int32))
    input_grad = total.astype(jnp.bfloat16)
    weight_grad = jnp.dot(context.T, out_grad, preferred_element_type=jnp.float32).astype(jnp.bfloat16)
    return (input_grad, weight_grad)
```

```python
import jax
import jax.numpy as jnp
from jax import lax
from jax.experimental import pallas as pl
from jax.experimental.pallas import tpu as pltpu
from jax.sharding import PartitionSpec as P

VMEM_BYTES = 48 * 1024 * 1024


def partial_block(dest, grads, weight, after, tile):
    tokens, width = grads.shape

    def kernel(dest_ref, grads_ref, weight_ref, *refs):
        outs = refs[len(after):]
        step = pl.program_id(0)
        value = lax.dot_general(
            grads_ref[...], weight_ref[...], (((1,), (1,)), ((), ())), preferred_element_type=jnp.float32
        ).astype(jnp.bfloat16)
        for place in range(3):
            @pl.when(step // 2 == place)
            def _():
                outs[place][...] = value

    def out_spec(place):
        return pl.BlockSpec((tokens, tile), lambda i, dest_ref: (0, jnp.clip(i - 2 * place, 0, 1)))

    return pl.pallas_call(
        kernel,
        grid_spec=pltpu.PrefetchScalarGridSpec(
            num_scalar_prefetch=1,
            grid=(6,),
            in_specs=[
                pl.BlockSpec((tokens, width), lambda i, dest_ref: (0, 0)),
                pl.BlockSpec((tile, width), lambda i, dest_ref: (dest_ref[i], 0)),
            ] + [pl.BlockSpec(memory_space=pl.ANY)] * len(after),
            out_specs=[out_spec(place) for place in range(3)],
        ),
        out_shape=[jax.ShapeDtypeStruct((tokens, 2 * tile), jnp.bfloat16)] * 3,
        compiler_params=pltpu.CompilerParams(vmem_limit_bytes=VMEM_BYTES),
        cost_estimate=pl.CostEstimate(
            flops=12 * tokens * width * tile, bytes_accessed=2 * (tokens * width + 6 * tile * (width + tokens)), transcendentals=0
        ),
        name="partial_input_grad",
    )(dest, grads, weight, *after)


def weight_grad_rows(dest, parts, grads, total, rows, tile):
    tokens, width = grads.shape

    def kernel(dest_ref, first_ref, second_ref, third_ref, grads_ref, *refs):
        out_ref = refs[-1]
        step = pl.program_id(0)
        for place, part_ref in enumerate((first_ref, second_ref, third_ref)):
            @pl.when(step // 2 == place)
            def _():
                out_ref[...] = lax.dot_general(
                    part_ref[...], grads_ref[...], (((0,), (0,)), ((), ())), preferred_element_type=jnp.float32
                ).astype(jnp.bfloat16)

    def part_spec(place):
        return pl.BlockSpec((tokens, tile), lambda i, dest_ref: (0, jnp.clip(i - 2 * place, 0, 1)))

    earlier = [] if total is None else [total]
    return pl.pallas_call(
        kernel,
        grid_spec=pltpu.PrefetchScalarGridSpec(
            num_scalar_prefetch=1,
            grid=(6,),
            in_specs=[part_spec(place) for place in range(3)]
            + [pl.BlockSpec((tokens, width), lambda i, dest_ref: (0, 0))]
            + [pl.BlockSpec(memory_space=pl.ANY)] * len(earlier),
            out_specs=pl.BlockSpec((tile, width), lambda i, dest_ref: (dest_ref[i], 0)),
        ),
        out_shape=jax.ShapeDtypeStruct((rows, width), jnp.bfloat16),
        input_output_aliases={5: 0} if earlier else {},
        compiler_params=pltpu.CompilerParams(vmem_limit_bytes=VMEM_BYTES),
        cost_estimate=pl.CostEstimate(
            flops=12 * tokens * width * tile, bytes_accessed=2 * (tokens * width + 6 * tile * (width + tokens)), transcendentals=0
        ),
        name="weight_grad",
    )(dest, *parts, grads, *earlier)


def add(*values):
    return sum(value.astype(jnp.float32) for value in values).astype(jnp.bfloat16)


def grid_per_device(context, out_grad, weight):
    own_row = lax.axis_index("row")
    column = lax.axis_index("col")
    z, y = column // 2, column % 2
    tokens, features = context.shape
    tile = features // 3
    middle = (z == 1) | (z == 2)

    pairs_pair = [(c, c ^ 2) for c in range(8)]
    pairs_middle = [(c, c ^ 6) for c in range(2, 6)]
    pairs_y = [(c, c ^ 1) for c in range(8)]
    swap_z = lambda value: lax.ppermute(value, "col", pairs_pair)
    swap_middle = lambda value: lax.ppermute(value, "col", pairs_middle)
    swap_y = lambda value: lax.ppermute(value, "col", pairs_y)
    pick = lambda on_middle, on_end: jnp.where(middle, on_middle, on_end)

    far_end = jnp.where(z < 2, 3, 0)
    far_middle = jnp.where(z < 2, 2, 1)

    def blocks(at, order):
        own, other = 3 * (2 * at + y), 3 * (2 * at + 1 - y)
        base = {"own": own, "other": other}
        return jnp.stack([base[name] + index for name, index in order]).astype(jnp.int32)

    partial_order = (("other", 1), ("other", 2), ("own", 1), ("own", 2), ("own", 0), ("other", 0))
    grad_order = (("own", 1), ("own", 2), ("own", 0), ("other", 0), ("other", 1), ("other", 2))

    other_grads = lax.ppermute(out_grad, "row", [(0, 1), (1, 0)])
    context_a, context_b = context[:, :tile], context[:, tile:]
    other_a = swap_y(context_a)
    near_b = swap_z(context_b)
    mid_b = swap_middle(context_b)
    other_b = swap_y(context_b)

    grads = jnp.where(
        own_row == 0, jnp.concatenate([out_grad, other_grads]), jnp.concatenate([other_grads, out_grad])
    )

    def partials(at, after):
        return partial_block(blocks(at, partial_order), grads, weight, after, tile)

    send1, own1, both1 = partials(far_end, ())
    here_a = jnp.concatenate([context_a, other_a], axis=1)
    near_a = swap_z(here_a)
    mid_a = swap_middle(here_a)
    own1 = add(own1, swap_y(send1))
    z3 = swap_z(pick(mid_b, both1))
    m3 = swap_middle(near_b)
    send2, own2, both2 = partials(far_middle, (near_b,))
    near_other_b = swap_y(near_b)
    z4 = swap_z(pick(mid_a, own1))
    m4 = swap_middle(near_a)
    total = weight_grad_rows(blocks(z, grad_order), (context_b, here_a, other_b), grads, None, weight.shape[0], tile)
    own2 = add(own2, swap_y(send2))
    fm_b = pick(mid_b, z3)
    z5 = swap_z(pick(m3, both2))
    m5 = swap_middle(add(both1, z3))
    fm_other_b = swap_y(fm_b)
    send3, own3, both3 = partials(z ^ 1, (z3,))
    total = weight_grad_rows(blocks(z ^ 1, grad_order), (near_b, near_a, near_other_b), grads, total, weight.shape[0], tile)
    fm_a = pick(mid_a, z4)
    z6 = swap_z(pick(m4, own2))
    m6 = swap_middle(add(own1, z4))
    own3 = add(own3, swap_y(send3))
    fe_b = pick(m3, z5)
    z7 = swap_z(add(both3, m5))
    m7 = swap_middle(add(both2, z5))
    fe_other_b = swap_y(fe_b)
    send4, own4, both4 = partials(z, (z5,))
    total = weight_grad_rows(blocks(far_middle, grad_order), (fm_b, fm_a, fm_other_b), grads, total, weight.shape[0], tile)
    fe_a = pick(m4, z6)
    z8 = swap_z(add(own3, m6))
    m8 = swap_middle(add(own2, z6))
    own4 = add(own4, swap_y(send4))
    total = weight_grad_rows(blocks(far_end, grad_order), (fe_b, fe_a, fe_other_b), grads, total, weight.shape[0], tile)
    ours = add(both4[:, :tile], z7[:, :tile], m7[:, :tile])
    theirs = add(both4[:, tile:], z7[:, tile:], m7[:, tile:])
    ours = add(ours, swap_y(theirs))
    input_grad = jnp.concatenate([ours, add(own4, z8, m8)], axis=1)
    return (input_grad, total)


def plain_per_device(context, out_grad, weight):
    all_grads = lax.all_gather(out_grad, "row", axis=0, tiled=True)
    gathered = lax.all_gather(context, "col", axis=1, tiled=True)
    weight_grad = lax.dot_general(
        gathered, all_grads, (((0,), (0,)), ((), ())), preferred_element_type=jnp.float32
    )
    partial_value = lax.dot_general(
        all_grads, weight, (((1,), (1,)), ((), ())), preferred_element_type=jnp.float32
    )
    input_grad = lax.psum_scatter(
        partial_value.astype(jnp.bfloat16), "col", scatter_dimension=1, tiled=True
    )
    return (input_grad, weight_grad.astype(jnp.bfloat16))


def solution(mesh):
    placed = (P("groups", ("row", "col")), P(("groups", "row"), "col"), P("row", "col"))
    on_grid = mesh.shape["col"] == 8 and mesh.shape["row"] == 2
    return jax.shard_map(
        grid_per_device if on_grid else plain_per_device,
        mesh=mesh,
        in_specs=placed,
        out_specs=(P("groups", ("row", "col")), P(("groups", "row"), "col")),
        check_vma=False,
    )
```

```python
import jax
import jax.numpy as jnp
from jax import lax
from jax.experimental import pallas as pl
from jax.experimental.pallas import tpu as pltpu
from jax.sharding import PartitionSpec as P

VMEM_BYTES = 48 * 1024 * 1024
ANYWHERE = pl.BlockSpec(memory_space=pl.ANY)
AFTER = {
    "w1": ("X1",),
    "cross": ("w1",),
    "t3": ("cross",),
    "X2": ("t3",),
    "t4": ("X2",),
    "w2": ("t4", "y1",),
    "t5m": ("w2",),
    "ynf": ("t5m",),
    "X3": ("ynf",),
    "t5": ("t5m",),
    "t6m": ("X3", "t5",),
    "t6": ("t6m",),
    "fma": ("t6m",),
    "X4": ("t6",),
    "t7": ("X4",),
    "t7m": ("t7",),
    "feb": ("t7m",),
    "w3": ("t7m",),
    "t8m": ("w3",),
    "fea": ("t8m",),
    "t8": ("t8m",),
    "ylast": ("t8m",),
    "w4": ("ylast",),
}


def cost(flops, moved):
    return pl.CostEstimate(flops=5 * flops // 2, bytes_accessed=5 * moved // 2, transcendentals=0)


def partial_blocks(dest, counts, grads, weight, arrived, tile):
    tokens, width = grads.shape
    halves = [count // 2 for count in counts]
    firsts = [sum(halves[:place]) for place in range(len(counts))]

    def kernel(dest_ref, grads_ref, one_ref, two_ref, *refs):
        outs = refs[len(arrived):]
        step = pl.program_id(0)

        def dot(weight_ref):
            return lax.dot_general(
                grads_ref[...], weight_ref[...], (((1,), (1,)), ((), ())), preferred_element_type=jnp.float32
            ).astype(jnp.bfloat16)

        one, two = dot(one_ref), dot(two_ref)
        for first, half, out_ref in zip(firsts, halves, outs):
            @pl.when((step >= first) & (step < first + half))
            def _():
                out_ref[:, :tile] = one
                out_ref[:, tile:] = two

    def out_spec(first, half):
        return pl.BlockSpec((tokens, 2 * tile), lambda i, dest_ref: (0, jnp.clip(i - first, 0, half - 1)))

    features = sum(counts) * tile
    return pl.pallas_call(
        kernel,
        grid_spec=pltpu.PrefetchScalarGridSpec(
            num_scalar_prefetch=1,
            grid=(sum(halves),),
            in_specs=[
                pl.BlockSpec((tokens, width), lambda i, dest_ref: (0, 0)),
                pl.BlockSpec((tile, width), lambda i, dest_ref: (dest_ref[2 * i], 0)),
                pl.BlockSpec((tile, width), lambda i, dest_ref: (dest_ref[2 * i + 1], 0)),
            ] + [ANYWHERE] * len(arrived),
            out_specs=[out_spec(first, half) for first, half in zip(firsts, halves)],
        ),
        out_shape=[pltpu.HBM((tokens, count * tile), jnp.bfloat16) for count in counts],
        compiler_params=pltpu.CompilerParams(vmem_limit_bytes=VMEM_BYTES),
        cost_estimate=cost(2 * tokens * width * features, 2 * (tokens * width + features * (width + tokens))),
        name="partial_input_grad",
    )(dest, grads, weight, weight, *arrived)


def weight_grad_rows(dest, parts, grads, total, rows, tile, arrived):
    tokens, width = grads.shape
    counts = [count for _, _, count in parts]
    begins = [sum(counts[:place]) for place in range(len(parts))]

    def kernel(dest_ref, *refs):
        grads_ref, out_ref = refs[len(parts)], refs[-1]
        step = pl.program_id(0)
        for begin, count, part_ref in zip(begins, counts, refs):
            @pl.when((step >= begin) & (step < begin + count))
            def _():
                out_ref[...] = lax.dot_general(
                    part_ref[...], grads_ref[...], (((0,), (0,)), ((), ())), preferred_element_type=jnp.float32
                ).astype(jnp.bfloat16)

    def part_spec(begin, first, count):
        return pl.BlockSpec((tokens, tile), lambda i, dest_ref: (0, first + jnp.clip(i - begin, 0, count - 1)))

    earlier = [] if total is None else [total]
    features = sum(counts) * tile
    return pl.pallas_call(
        kernel,
        grid_spec=pltpu.PrefetchScalarGridSpec(
            num_scalar_prefetch=1,
            grid=(sum(counts),),
            in_specs=[part_spec(begin, first, count) for begin, (_, first, count) in zip(begins, parts)]
            + [pl.BlockSpec((tokens, width), lambda i, dest_ref: (0, 0))]
            + [ANYWHERE] * (len(earlier) + len(arrived)),
            out_specs=pl.BlockSpec((tile, width), lambda i, dest_ref: (dest_ref[i], 0)),
        ),
        out_shape=jax.ShapeDtypeStruct((rows, width), jnp.bfloat16),
        input_output_aliases={len(parts) + 2: 0} if earlier else {},
        compiler_params=pltpu.CompilerParams(vmem_limit_bytes=VMEM_BYTES),
        cost_estimate=cost(2 * tokens * width * features, 2 * (tokens * width + features * (width + tokens))),
        name="weight_grad",
    )(dest, *(array for array, _, _ in parts), grads, *earlier, *arrived)


def combine(on_middle, arrays, outs, tile, arrived=()):
    tokens = arrays[0].shape[0]
    steps = 2
    rows = tokens // steps

    def kernel(middle_ref, *refs):
        out_refs = refs[len(arrays) + len(arrived):]

        def term(number, place):
            return refs[number][:, place * tile:(place + 1) * tile]

        def write(out_ref, place, terms):
            value = term(*terms[0])
            if len(terms) > 1:
                value = sum(term(*each).astype(jnp.float32) for each in terms).astype(jnp.bfloat16)
            out_ref[:, place * tile:(place + 1) * tile] = value

        for which in range(2):
            @pl.when(middle_ref[0] == 1 - which)
            def _():
                for out_ref, tiles in zip(out_refs, outs):
                    for place, terms in enumerate(tiles):
                        if isinstance(terms, tuple):
                            write(out_ref, place, terms[which])
        for out_ref, tiles in zip(out_refs, outs):
            for place, terms in enumerate(tiles):
                if not isinstance(terms, tuple):
                    write(out_ref, place, terms)

    def spec(width):
        return pl.BlockSpec((rows, width), lambda i, middle_ref: (i, 0))

    widths = [len(tiles) * tile for tiles in outs]
    moved = 2 * tokens * (sum(widths) + sum(array.shape[1] for array in arrays))
    return pl.pallas_call(
        kernel,
        grid_spec=pltpu.PrefetchScalarGridSpec(
            num_scalar_prefetch=1,
            grid=(steps,),
            in_specs=[spec(array.shape[1]) for array in arrays] + [ANYWHERE] * len(arrived),
            out_specs=[spec(width) for width in widths],
        ),
        out_shape=[pltpu.HBM((tokens, width), jnp.bfloat16) for width in widths],
        compiler_params=pltpu.CompilerParams(vmem_limit_bytes=VMEM_BYTES),
        cost_estimate=cost(moved, moved),
        name="combine",
    )(on_middle, *arrays, *arrived)


def each(*terms):
    return [[(number, first + place) for number, first in terms] for place in range(2)]


def either(on_middle, at_ends):
    return list(zip(each(*on_middle), each(*at_ends)))


def grid_per_device(context, out_grad, weight):
    own_row = lax.axis_index("row")
    column = lax.axis_index("col")
    z, y = column // 2, column % 2
    tile = context.shape[1] // 3
    middle = ((z == 1) | (z == 2)).astype(jnp.int32).reshape(1)

    pairs_z = [(c, c ^ 2) for c in range(8)]
    pairs_middle = [(c, c ^ 6) for c in range(2, 6)]
    pairs_y = [(c, c ^ 1) for c in range(8)]
    swap_z = lambda value: lax.ppermute(value, "col", pairs_z)
    swap_middle = lambda value: lax.ppermute(value, "col", pairs_middle)
    swap_y = lambda value: lax.ppermute(value, "col", pairs_y)

    near, far_end, far_middle = z ^ 1, jnp.where(z < 2, 3, 0), jnp.where(z < 2, 2, 1)
    there = {}

    def arrived(name):
        return tuple(there[each] for each in AFTER.get(name, ()))

    def blocks(tiles):
        where = {"own": y, "other": 1 - y}
        return jnp.stack([3 * (2 * at + where[side]) + index for at, side, index in tiles]).astype(jnp.int32)

    def own(at, *tiles):
        return tuple((at, "own", index) for index in tiles)

    def other(at, *tiles):
        return tuple((at, "other", index) for index in tiles)

    def perm(name, value):
        there[name] = {"z": swap_z, "m": swap_middle, "y": swap_y}[name[0]](value)
        return there[name]

    def partials(name, places):
        tiles, counts = (), [2 * len(places)]
        for at in places:
            tiles += other(at, 1, 2)
        for at in places:
            tiles += own(at, 1, 2) + own(at, 0) + other(at, 0)
            counts += [2, 2]
        results = partial_blocks(blocks(tiles), counts, grads, weight, arrived(name), tile)
        there[name] = results[-1]
        return results

    def add_rows(name, tiles, parts, total):
        there[name] = weight_grad_rows(blocks(tiles), parts, grads, total, weight.shape[0], tile, arrived(name))
        return there[name]

    def mix(name, arrays, outs):
        results = combine(middle, arrays, outs, tile, arrived(name))
        there[name] = results[0]
        return results

    other_grads = lax.ppermute(out_grad, "row", [(0, 1), (1, 0)])
    other_c = perm("yC", context)
    near_c = perm("zC", context)
    mid_c = perm("mC", context)
    grads = jnp.where(
        own_row == 0, jnp.concatenate([out_grad, other_grads]), jnp.concatenate([other_grads, out_grad])
    )
    send1, own1, both1 = partials("X1", [far_end])
    got1 = perm("y1", send1)
    total = add_rows("w1", own(z, 0, 1, 2), [(context, 0, 3)], None)
    (cross,) = mix("cross", [other_c], [[[(0, 0)]]])
    near_x, mid_x = perm("zx", cross), perm("mx", cross)
    t3, near_b = mix("t3", [mid_c, both1, near_c], [either([(0, 1)], [(1, 0)]), each((2, 1))])
    z3, m3 = perm("z3", t3), perm("m3", near_b)
    send2, own2, both2 = partials("X2", [far_middle])
    near_a, t4, more_cross = mix("t4",
        [near_c, near_x, mid_c, mid_x, both2, other_c],
        [[[(0, 0)], [(1, 0)]], [([(2, 0)], [(4, 0)]), ([(3, 0)], [(4, 1)])], [[(5, 1)]]],
    )
    z4, m4 = perm("z4", t4), perm("m4", near_a)
    got2 = perm("y2", send2)
    total = add_rows("w2",
        other(z, 0, 1, 2) + own(near, 0, 1, 2) + other(near, 0),
        [(other_c, 0, 3), (near_c, 0, 3), (near_x, 0, 1)], total,
    )
    (t5m,) = mix("t5m", [both1, z3], [each((0, 0), (1, 0))])
    m5 = perm("m5", t5m)
    (y_nf,) = mix("ynf", [z3, near_c, mid_c], [[[(1, 2)]] + either([(2, 1)], [(0, 0)])])
    got_nf = perm("ynf_", y_nf)
    send3, own3, both3 = partials("X3", [near])
    got3 = perm("y3", send3)
    (t5,) = mix("t5", [m3, own1, got1], [either([(0, 0)], [(1, 0), (2, 0)])])
    z5 = perm("z5", t5)
    (t6m,) = mix("t6m", [both2, z4], [each((0, 0), (1, 0))])
    m6 = perm("m6", t6m)
    (t6,) = mix("t6", [m4, own2, got2], [either([(0, 0)], [(1, 0), (2, 0)])])
    z6 = perm("z6", t6)
    (fm_a,) = mix("fma", [z4, mid_c, mid_x], [[([(1, 0)], [(0, 0)]), ([(2, 0)], [(0, 1)])]])
    send4, own4, both4 = partials("X4", [z])
    (t7,) = mix("t7", [both3, m5], [each((0, 0), (1, 0))])
    z7 = perm("z7", t7)
    (t7m,) = mix("t7m", [own1, got1, z5], [each((0, 0), (1, 0), (2, 0))])
    m7 = perm("m7", t7m)
    (fe_b,) = mix("feb", [z5, m3], [either([(1, 0)], [(0, 0)])])
    fe_other_b = perm("yfe", fe_b)
    total = add_rows("w3",
        other(near, 2) + other(far_middle, 1, 2) + own(far_middle, 1, 2, 0) + other(far_middle, 0),
        [(got_nf, 0, 3), (y_nf, 1, 2), (fm_a, 0, 2)], total,
    )
    (t8m,) = mix("t8m", [own2, got2, z6], [each((0, 0), (1, 0), (2, 0))])
    m8 = perm("m8", t8m)
    near_cross = perm("zn", more_cross)
    (fe_a,) = mix("fea", [z6, m4], [either([(1, 0)], [(0, 0)])])
    (t8,) = mix("t8", [own3, got3, m7], [each((0, 0), (1, 0), (2, 0))])
    z8 = perm("z8", t8)
    got4 = perm("y4", send4)
    (theirs,) = mix("ylast", [both4, z7, m6], [[[(0, 1), (1, 1), (2, 1)]]])
    fin = perm("yfin", theirs)
    total = add_rows("w4",
        own(far_end, 1, 2, 0) + other(far_end, 0, 1, 2) + other(near, 1),
        [(fe_b, 0, 2), (fe_a, 0, 2), (fe_other_b, 0, 2), (near_cross, 0, 1)], total,
    )
    (input_grad,) = mix("final",
        [both4, z7, m6, fin, own4, z8, m8, got4],
        [[[(0, 0), (1, 0), (2, 0), (3, 0)]] + each((4, 0), (7, 0), (5, 0), (6, 0))],
    )
    return (input_grad, total)


def plain_per_device(context, out_grad, weight):
    all_grads = lax.all_gather(out_grad, "row", axis=0, tiled=True)
    gathered = lax.all_gather(context, "col", axis=1, tiled=True)
    weight_grad = lax.dot_general(
        gathered, all_grads, (((0,), (0,)), ((), ())), preferred_element_type=jnp.float32
    )
    partial_value = lax.dot_general(
        all_grads, weight, (((1,), (1,)), ((), ())), preferred_element_type=jnp.float32
    )
    input_grad = lax.psum_scatter(
        partial_value.astype(jnp.bfloat16), "col", scatter_dimension=1, tiled=True
    )
    return (input_grad, weight_grad.astype(jnp.bfloat16))


def solution(mesh):
    placed = (P("groups", ("row", "col")), P(("groups", "row"), "col"), P("row", "col"))
    on_grid = mesh.shape["col"] == 8 and mesh.shape["row"] == 2
    return jax.shard_map(
        grid_per_device if on_grid else plain_per_device,
        mesh=mesh,
        in_specs=placed,
        out_specs=(P("groups", ("row", "col")), P(("groups", "row"), "col")),
        check_vma=False,
    )
```

```python
import jax
import jax.numpy as jnp
from jax import lax
from jax.experimental import pallas as pl
from jax.experimental.pallas import tpu as pltpu
from jax.sharding import PartitionSpec as P

VMEM_BYTES = 48 * 1024 * 1024
ANYWHERE = pl.BlockSpec(memory_space=pl.ANY)
AFTER = {
    "w1": ("X12",),
    "t3": ("w1",),
    "t4": ("t3",),
    "w2": ("t4",),
    "t5m": ("w2",),
    "ynf": ("t5m",),
    "X3": ("ynf",),
    "t5": ("t5m",),
    "t6m": ("X3", "t5",),
    "t6": ("t6m",),
    "fma": ("t6m",),
    "X4": ("t6",),
    "t7": ("X4",),
    "t7m": ("t7",),
    "feb": ("t7m",),
    "w3": ("t7m",),
    "t8m": ("w3",),
    "fea": ("t8m",),
    "t8": ("t8m",),
    "ylast": ("t8m",),
    "w4": ("ylast",),
    "split": ("row",),
}


def cost(flops, moved):
    return pl.CostEstimate(flops=5 * flops // 2, bytes_accessed=5 * moved // 2, transcendentals=0)


def partial_blocks(dest, counts, grads, weight, arrived, tile):
    tokens, width = grads.shape
    halves = [count // 2 for count in counts]
    firsts = [sum(halves[:place]) for place in range(len(counts))]

    def kernel(dest_ref, grads_ref, one_ref, two_ref, *refs):
        outs = refs[len(arrived):]
        step = pl.program_id(0)

        def dot(weight_ref):
            return lax.dot_general(
                grads_ref[...], weight_ref[...], (((1,), (1,)), ((), ())), preferred_element_type=jnp.float32
            ).astype(jnp.bfloat16)

        one, two = dot(one_ref), dot(two_ref)
        for first, half, out_ref in zip(firsts, halves, outs):
            @pl.when((step >= first) & (step < first + half))
            def _():
                out_ref[:, :tile] = one
                out_ref[:, tile:] = two

    def out_spec(first, half):
        return pl.BlockSpec((tokens, 2 * tile), lambda i, dest_ref: (0, jnp.clip(i - first, 0, half - 1)))

    features = sum(counts) * tile
    return pl.pallas_call(
        kernel,
        grid_spec=pltpu.PrefetchScalarGridSpec(
            num_scalar_prefetch=1,
            grid=(sum(halves),),
            in_specs=[
                pl.BlockSpec((tokens, width), lambda i, dest_ref: (0, 0)),
                pl.BlockSpec((tile, width), lambda i, dest_ref: (dest_ref[2 * i], 0)),
                pl.BlockSpec((tile, width), lambda i, dest_ref: (dest_ref[2 * i + 1], 0)),
            ] + [ANYWHERE] * len(arrived),
            out_specs=[out_spec(first, half) for first, half in zip(firsts, halves)],
        ),
        out_shape=[pltpu.HBM((tokens, count * tile), jnp.bfloat16) for count in counts],
        compiler_params=pltpu.CompilerParams(vmem_limit_bytes=VMEM_BYTES),
        cost_estimate=cost(2 * tokens * width * features, 2 * (tokens * width + features * (width + tokens))),
        name="partial_input_grad",
    )(dest, grads, weight, weight, *arrived)


def weight_grad_rows(dest, parts, grads, total, rows, tile, arrived):
    tokens, width = grads.shape
    counts = [count for _, _, count in parts]
    begins = [sum(counts[:place]) for place in range(len(parts))]

    def kernel(dest_ref, *refs):
        grads_ref, out_ref = refs[len(parts)], refs[-1]
        step = pl.program_id(0)
        for begin, count, part_ref in zip(begins, counts, refs):
            @pl.when((step >= begin) & (step < begin + count))
            def _():
                out_ref[...] = lax.dot_general(
                    part_ref[...], grads_ref[...], (((0,), (0,)), ((), ())), preferred_element_type=jnp.float32
                ).astype(jnp.bfloat16)

    def part_spec(begin, first, count):
        return pl.BlockSpec((tokens, tile), lambda i, dest_ref: (0, first + jnp.clip(i - begin, 0, count - 1)))

    earlier = [] if total is None else [total]
    features = sum(counts) * tile
    return pl.pallas_call(
        kernel,
        grid_spec=pltpu.PrefetchScalarGridSpec(
            num_scalar_prefetch=1,
            grid=(sum(counts),),
            in_specs=[part_spec(begin, first, count) for begin, (_, first, count) in zip(begins, parts)]
            + [pl.BlockSpec((tokens, width), lambda i, dest_ref: (0, 0))]
            + [ANYWHERE] * (len(earlier) + len(arrived)),
            out_specs=pl.BlockSpec((tile, width), lambda i, dest_ref: (dest_ref[i], 0)),
        ),
        out_shape=jax.ShapeDtypeStruct((rows, width), jnp.bfloat16),
        input_output_aliases={len(parts) + 2: 0} if earlier else {},
        compiler_params=pltpu.CompilerParams(vmem_limit_bytes=VMEM_BYTES),
        cost_estimate=cost(2 * tokens * width * features, 2 * (tokens * width + features * (width + tokens))),
        name="weight_grad",
    )(dest, *(array for array, _, _ in parts), grads, *earlier, *arrived)


def combine(on_middle, arrays, outs, tile, arrived=()):
    tokens = arrays[0].shape[0]
    steps = 2
    rows = tokens // steps

    def kernel(middle_ref, *refs):
        out_refs = refs[len(arrays) + len(arrived):]

        def term(number, place):
            return refs[number][:, place * tile:(place + 1) * tile]

        def write(out_ref, place, terms):
            value = term(*terms[0])
            if len(terms) > 1:
                value = sum(term(*each).astype(jnp.float32) for each in terms).astype(jnp.bfloat16)
            out_ref[:, place * tile:(place + 1) * tile] = value

        for which in range(2):
            @pl.when(middle_ref[0] == 1 - which)
            def _():
                for out_ref, tiles in zip(out_refs, outs):
                    for place, terms in enumerate(tiles):
                        if isinstance(terms, tuple):
                            write(out_ref, place, terms[which])
        for out_ref, tiles in zip(out_refs, outs):
            for place, terms in enumerate(tiles):
                if not isinstance(terms, tuple):
                    write(out_ref, place, terms)

    def spec(width):
        return pl.BlockSpec((rows, width), lambda i, middle_ref: (i, 0))

    widths = [len(tiles) * tile for tiles in outs]
    moved = 2 * tokens * (sum(widths) + sum(array.shape[1] for array in arrays))
    return pl.pallas_call(
        kernel,
        grid_spec=pltpu.PrefetchScalarGridSpec(
            num_scalar_prefetch=1,
            grid=(steps,),
            in_specs=[spec(array.shape[1]) for array in arrays] + [ANYWHERE] * len(arrived),
            out_specs=[spec(width) for width in widths],
        ),
        out_shape=[pltpu.HBM((tokens, width), jnp.bfloat16) for width in widths],
        compiler_params=pltpu.CompilerParams(vmem_limit_bytes=VMEM_BYTES),
        cost_estimate=cost(moved, moved),
        name="combine",
    )(on_middle, *arrays, *arrived)


def each(*terms):
    return [[(number, first + place) for number, first in terms] for place in range(2)]


def either(on_middle, at_ends):
    return list(zip(each(*on_middle), each(*at_ends)))


def grid_per_device(context, out_grad, weight):
    own_row = lax.axis_index("row")
    column = lax.axis_index("col")
    z, y = column // 2, column % 2
    tile = context.shape[1] // 3
    middle = ((z == 1) | (z == 2)).astype(jnp.int32).reshape(1)

    pairs_z = [(c, c ^ 2) for c in range(8)]
    pairs_middle = [(c, c ^ 6) for c in range(2, 6)]
    pairs_y = [(c, c ^ 1) for c in range(8)]
    swap_z = lambda value: lax.ppermute(value, "col", pairs_z)
    swap_middle = lambda value: lax.ppermute(value, "col", pairs_middle)
    swap_y = lambda value: lax.ppermute(value, "col", pairs_y)

    near, far_end, far_middle = z ^ 1, jnp.where(z < 2, 3, 0), jnp.where(z < 2, 2, 1)
    there = {}

    def arrived(name):
        return tuple(there[each] for each in AFTER.get(name, ()))

    def blocks(tiles):
        where = {"own": y, "other": 1 - y}
        return jnp.stack([3 * (2 * at + where[side]) + index for at, side, index in tiles]).astype(jnp.int32)

    def own(at, *tiles):
        return tuple((at, "own", index) for index in tiles)

    def other(at, *tiles):
        return tuple((at, "other", index) for index in tiles)

    def perm(name, value):
        there[name] = {"z": swap_z, "m": swap_middle, "y": swap_y}[name[0]](value)
        return there[name]

    def partials(name, places):
        tiles, counts = (), [2 * len(places)]
        for at in places:
            tiles += other(at, 1, 2)
        for at in places:
            tiles += own(at, 1, 2) + own(at, 0) + other(at, 0)
            counts += [2, 2]
        results = partial_blocks(blocks(tiles), counts, grads, weight, arrived(name), tile)
        there[name] = results[-1]
        return results

    def add_rows(name, tiles, parts, total):
        there[name] = weight_grad_rows(blocks(tiles), parts, grads, total, weight.shape[0], tile, arrived(name))
        return there[name]

    def mix(name, arrays, outs):
        results = combine(middle, arrays, outs, tile, arrived(name))
        there[name] = results[0]
        return results

    other_grads = lax.ppermute(out_grad, "row", [(0, 1), (1, 0)])
    near_c = perm("zC", context)
    mid_c = perm("mC", context)
    there["row"] = other_grads
    context_0, context_12 = mix("split", [context], [[[(0, 0)]], each((0, 1))])
    other_c0 = perm("yC0", context_0)
    other_c = perm("yC", context_12)
    grads = jnp.where(
        own_row == 0, jnp.concatenate([out_grad, other_grads]), jnp.concatenate([other_grads, out_grad])
    )
    send12, own1, both1, own2, both2 = partials("X12", [far_end, far_middle])
    got12 = perm("y12", send12)
    total = add_rows("w1", own(z, 0, 1, 2), [(context, 0, 3)], None)
    near_x, mid_x = perm("zx", other_c0), perm("mx", other_c0)
    t3, near_b = mix("t3", [mid_c, both1, near_c], [either([(0, 1)], [(1, 0)]), each((2, 1))])
    z3, m3 = perm("z3", t3), perm("m3", near_b)
    near_a, t4 = mix("t4",
        [near_c, near_x, mid_c, mid_x, both2],
        [[[(0, 0)], [(1, 0)]], [([(2, 0)], [(4, 0)]), ([(3, 0)], [(4, 1)])]],
    )
    z4, m4 = perm("z4", t4), perm("m4", near_a)
    total = add_rows("w2", other(z, 0, 1, 2) + other(near, 0), [(other_c0, 0, 1), (other_c, 0, 2), (near_x, 0, 1)], total)
    (t5m,) = mix("t5m", [both1, z3], [each((0, 0), (1, 0))])
    m5 = perm("m5", t5m)
    (y_nf,) = mix("ynf", [z3, near_c, mid_c], [[[(1, 2)]] + either([(2, 1)], [(0, 0)])])
    got_nf = perm("ynf_", y_nf)
    send3, own3, both3 = partials("X3", [near])
    got3 = perm("y3", send3)
    (t5,) = mix("t5", [m3, own1, got12], [either([(0, 0)], [(1, 0), (2, 0)])])
    z5 = perm("z5", t5)
    (t6m,) = mix("t6m", [both2, z4], [each((0, 0), (1, 0))])
    m6 = perm("m6", t6m)
    (t6,) = mix("t6", [m4, own2, got12], [either([(0, 0)], [(1, 0), (2, 2)])])
    z6 = perm("z6", t6)
    (fm_a,) = mix("fma", [z4, mid_c, mid_x], [[([(1, 0)], [(0, 0)]), ([(2, 0)], [(0, 1)])]])
    send4, own4, both4 = partials("X4", [z])
    (t7,) = mix("t7", [both3, m5], [each((0, 0), (1, 0))])
    z7 = perm("z7", t7)
    (t7m,) = mix("t7m", [own1, got12, z5], [each((0, 0), (1, 0), (2, 0))])
    m7 = perm("m7", t7m)
    (fe_b,) = mix("feb", [z5, m3], [either([(1, 0)], [(0, 0)])])
    fe_other_b = perm("yfe", fe_b)
    total = add_rows("w3",
        own(near, 0, 1, 2) + other(near, 2) + other(far_middle, 1, 2) + own(far_middle, 1, 2, 0) + other(far_middle, 0),
        [(near_c, 0, 3), (got_nf, 0, 3), (y_nf, 1, 2), (fm_a, 0, 2)], total,
    )
    t8m, more_cross = mix("t8m", [own2, got12, z6, other_c], [each((0, 0), (1, 2), (2, 0)), [[(3, 0)]]])
    m8 = perm("m8", t8m)
    near_cross = perm("zn", more_cross)
    (fe_a,) = mix("fea", [z6, m4], [either([(1, 0)], [(0, 0)])])
    (t8,) = mix("t8", [own3, got3, m7], [each((0, 0), (1, 0), (2, 0))])
    z8 = perm("z8", t8)
    got4 = perm("y4", send4)
    (theirs,) = mix("ylast", [both4, z7, m6], [[[(0, 1), (1, 1), (2, 1)]]])
    fin = perm("yfin", theirs)
    total = add_rows("w4",
        own(far_end, 1, 2, 0) + other(far_end, 0, 1, 2) + other(near, 1),
        [(fe_b, 0, 2), (fe_a, 0, 2), (fe_other_b, 0, 2), (near_cross, 0, 1)], total,
    )
    (input_grad,) = mix("final",
        [both4, z7, m6, fin, own4, z8, m8, got4],
        [[[(0, 0), (1, 0), (2, 0), (3, 0)]] + each((4, 0), (7, 0), (5, 0), (6, 0))],
    )
    return (input_grad, total)


def plain_per_device(context, out_grad, weight):
    all_grads = lax.all_gather(out_grad, "row", axis=0, tiled=True)
    gathered = lax.all_gather(context, "col", axis=1, tiled=True)
    weight_grad = lax.dot_general(
        gathered, all_grads, (((0,), (0,)), ((), ())), preferred_element_type=jnp.float32
    )
    partial_value = lax.dot_general(
        all_grads, weight, (((1,), (1,)), ((), ())), preferred_element_type=jnp.float32
    )
    input_grad = lax.psum_scatter(
        partial_value.astype(jnp.bfloat16), "col", scatter_dimension=1, tiled=True
    )
    return (input_grad, weight_grad.astype(jnp.bfloat16))


def solution(mesh):
    placed = (P("groups", ("row", "col")), P(("groups", "row"), "col"), P("row", "col"))
    on_grid = mesh.shape["col"] == 8 and mesh.shape["row"] == 2
    return jax.shard_map(
        grid_per_device if on_grid else plain_per_device,
        mesh=mesh,
        in_specs=placed,
        out_specs=(P("groups", ("row", "col")), P(("groups", "row"), "col")),
        check_vma=False,
    )
```

```python
import jax
import jax.numpy as jnp
from jax import lax
from jax.experimental import pallas as pl
from jax.experimental.pallas import tpu as pltpu
from jax.sharding import PartitionSpec as P

VMEM_BYTES = 48 * 1024 * 1024
ANYWHERE = pl.BlockSpec(memory_space=pl.ANY)
AFTER = {
    "w1": ("X12",),
    "t3": ("w1",),
    "t4": ("t3",),
    "w2": ("t4",),
    "t5m": ("w2",),
    "ynf": ("t5m",),
    "X3": ("ynf",),
    "t5": ("t5m",),
    "t6m": ("X3", "t5",),
    "t6": ("t6m",),
    "fma": ("t6m",),
    "X4": ("t6",),
    "t7": ("X4",),
    "t7m": ("t7",),
    "feb": ("t7m",),
    "w3": ("t7m",),
    "t8m": ("w3",),
    "fea": ("t8m",),
    "t8": ("t8m",),
    "ylast": ("t8m",),
    "w4": ("ylast",),
    "split": ("row",),
    "early": ("w4",),
}


def cost(flops, moved):
    return pl.CostEstimate(flops=5 * flops // 2, bytes_accessed=5 * moved // 2, transcendentals=0)


def partial_blocks(dest, counts, grads, weight, arrived, tile):
    tokens, width = grads.shape
    halves = [count // 2 for count in counts]
    firsts = [sum(halves[:place]) for place in range(len(counts))]

    def kernel(dest_ref, grads_ref, one_ref, two_ref, *refs):
        outs = refs[len(arrived):]
        step = pl.program_id(0)

        def dot(weight_ref):
            return lax.dot_general(
                grads_ref[...], weight_ref[...], (((1,), (1,)), ((), ())), preferred_element_type=jnp.float32
            ).astype(jnp.bfloat16)

        one, two = dot(one_ref), dot(two_ref)
        for first, half, out_ref in zip(firsts, halves, outs):
            @pl.when((step >= first) & (step < first + half))
            def _():
                out_ref[:, :tile] = one
                out_ref[:, tile:] = two

    def out_spec(first, half):
        return pl.BlockSpec((tokens, 2 * tile), lambda i, dest_ref: (0, jnp.clip(i - first, 0, half - 1)))

    features = sum(counts) * tile
    return pl.pallas_call(
        kernel,
        grid_spec=pltpu.PrefetchScalarGridSpec(
            num_scalar_prefetch=1,
            grid=(sum(halves),),
            in_specs=[
                pl.BlockSpec((tokens, width), lambda i, dest_ref: (0, 0)),
                pl.BlockSpec((tile, width), lambda i, dest_ref: (dest_ref[2 * i], 0)),
                pl.BlockSpec((tile, width), lambda i, dest_ref: (dest_ref[2 * i + 1], 0)),
            ] + [ANYWHERE] * len(arrived),
            out_specs=[out_spec(first, half) for first, half in zip(firsts, halves)],
        ),
        out_shape=[pltpu.HBM((tokens, count * tile), jnp.bfloat16) for count in counts],
        compiler_params=pltpu.CompilerParams(vmem_limit_bytes=VMEM_BYTES),
        cost_estimate=cost(2 * tokens * width * features, 2 * (tokens * width + features * (width + tokens))),
        name="partial_input_grad",
    )(dest, grads, weight, weight, *arrived)


def weight_grad_rows(dest, parts, grads, total, rows, tile, arrived):
    tokens, width = grads.shape
    counts = [count for _, _, count in parts]
    begins = [sum(counts[:place]) for place in range(len(parts))]

    def kernel(dest_ref, *refs):
        grads_ref, out_ref = refs[len(parts)], refs[-1]
        step = pl.program_id(0)
        for begin, count, part_ref in zip(begins, counts, refs):
            @pl.when((step >= begin) & (step < begin + count))
            def _():
                out_ref[...] = lax.dot_general(
                    part_ref[...], grads_ref[...], (((0,), (0,)), ((), ())), preferred_element_type=jnp.float32
                ).astype(jnp.bfloat16)

    def part_spec(begin, first, count):
        return pl.BlockSpec((tokens, tile), lambda i, dest_ref: (0, first + jnp.clip(i - begin, 0, count - 1)))

    earlier = [] if total is None else [total]
    features = sum(counts) * tile
    return pl.pallas_call(
        kernel,
        grid_spec=pltpu.PrefetchScalarGridSpec(
            num_scalar_prefetch=1,
            grid=(sum(counts),),
            in_specs=[part_spec(begin, first, count) for begin, (_, first, count) in zip(begins, parts)]
            + [pl.BlockSpec((tokens, width), lambda i, dest_ref: (0, 0))]
            + [ANYWHERE] * (len(earlier) + len(arrived)),
            out_specs=pl.BlockSpec((tile, width), lambda i, dest_ref: (dest_ref[i], 0)),
        ),
        out_shape=jax.ShapeDtypeStruct((rows, width), jnp.bfloat16),
        input_output_aliases={len(parts) + 2: 0} if earlier else {},
        compiler_params=pltpu.CompilerParams(vmem_limit_bytes=VMEM_BYTES),
        cost_estimate=cost(2 * tokens * width * features, 2 * (tokens * width + features * (width + tokens))),
        name="weight_grad",
    )(dest, *(array for array, _, _ in parts), grads, *earlier, *arrived)


def combine(on_middle, arrays, outs, tile, arrived=()):
    tokens = arrays[0].shape[0]
    steps = 2
    rows = tokens // steps

    def kernel(middle_ref, *refs):
        out_refs = refs[len(arrays) + len(arrived):]

        def term(number, place):
            return refs[number][:, place * tile:(place + 1) * tile]

        def write(out_ref, place, terms):
            value = term(*terms[0])
            if len(terms) > 1:
                value = sum(term(*each).astype(jnp.float32) for each in terms).astype(jnp.bfloat16)
            out_ref[:, place * tile:(place + 1) * tile] = value

        for which in range(2):
            @pl.when(middle_ref[0] == 1 - which)
            def _():
                for out_ref, tiles in zip(out_refs, outs):
                    for place, terms in enumerate(tiles):
                        if isinstance(terms, tuple):
                            write(out_ref, place, terms[which])
        for out_ref, tiles in zip(out_refs, outs):
            for place, terms in enumerate(tiles):
                if not isinstance(terms, tuple):
                    write(out_ref, place, terms)

    def spec(width):
        return pl.BlockSpec((rows, width), lambda i, middle_ref: (i, 0))

    widths = [len(tiles) * tile for tiles in outs]
    moved = 2 * tokens * (sum(widths) + sum(array.shape[1] for array in arrays))
    return pl.pallas_call(
        kernel,
        grid_spec=pltpu.PrefetchScalarGridSpec(
            num_scalar_prefetch=1,
            grid=(steps,),
            in_specs=[spec(array.shape[1]) for array in arrays] + [ANYWHERE] * len(arrived),
            out_specs=[spec(width) for width in widths],
        ),
        out_shape=[pltpu.HBM((tokens, width), jnp.bfloat16) for width in widths],
        compiler_params=pltpu.CompilerParams(vmem_limit_bytes=VMEM_BYTES),
        cost_estimate=cost(moved, moved),
        name="combine",
    )(on_middle, *arrays, *arrived)


def each(*terms):
    return [[(number, first + place) for number, first in terms] for place in range(2)]


def either(on_middle, at_ends):
    return list(zip(each(*on_middle), each(*at_ends)))


def grid_per_device(context, out_grad, weight):
    own_row = lax.axis_index("row")
    column = lax.axis_index("col")
    z, y = column // 2, column % 2
    tile = context.shape[1] // 3
    middle = ((z == 1) | (z == 2)).astype(jnp.int32).reshape(1)

    pairs_z = [(c, c ^ 2) for c in range(8)]
    pairs_middle = [(c, c ^ 6) for c in range(2, 6)]
    pairs_y = [(c, c ^ 1) for c in range(8)]
    swap_z = lambda value: lax.ppermute(value, "col", pairs_z)
    swap_middle = lambda value: lax.ppermute(value, "col", pairs_middle)
    swap_y = lambda value: lax.ppermute(value, "col", pairs_y)

    near, far_end, far_middle = z ^ 1, jnp.where(z < 2, 3, 0), jnp.where(z < 2, 2, 1)
    there = {}

    def arrived(name):
        return tuple(there[each] for each in AFTER.get(name, ()))

    def blocks(tiles):
        where = {"own": y, "other": 1 - y}
        return jnp.stack([3 * (2 * at + where[side]) + index for at, side, index in tiles]).astype(jnp.int32)

    def own(at, *tiles):
        return tuple((at, "own", index) for index in tiles)

    def other(at, *tiles):
        return tuple((at, "other", index) for index in tiles)

    def perm(name, value):
        there[name] = {"z": swap_z, "m": swap_middle, "y": swap_y}[name[0]](value)
        return there[name]

    def partials(name, places):
        tiles, counts = (), [2 * len(places)]
        for at in places:
            tiles += other(at, 1, 2)
        for at in places:
            tiles += own(at, 1, 2) + own(at, 0) + other(at, 0)
            counts += [2, 2]
        results = partial_blocks(blocks(tiles), counts, grads, weight, arrived(name), tile)
        there[name] = results[-1]
        return results

    def add_rows(name, tiles, parts, total):
        there[name] = weight_grad_rows(blocks(tiles), parts, grads, total, weight.shape[0], tile, arrived(name))
        return there[name]

    def mix(name, arrays, outs):
        results = combine(middle, arrays, outs, tile, arrived(name))
        there[name] = results[0]
        return results

    other_grads = lax.ppermute(out_grad, "row", [(0, 1), (1, 0)])
    near_c = perm("zC", context)
    mid_c = perm("mC", context)
    there["row"] = other_grads
    context_0, context_12 = mix("split", [context], [[[(0, 0)]], each((0, 1))])
    other_c0 = perm("yC0", context_0)
    other_c = perm("yC", context_12)
    grads = jnp.where(
        own_row == 0, jnp.concatenate([out_grad, other_grads]), jnp.concatenate([other_grads, out_grad])
    )
    send12, own1, both1, own2, both2 = partials("X12", [far_end, far_middle])
    got12 = perm("y12", send12)
    total = add_rows("w1", own(z, 0, 1, 2), [(context, 0, 3)], None)
    near_x, mid_x = perm("zx", other_c0), perm("mx", other_c0)
    t3, near_b = mix("t3", [mid_c, both1, near_c], [either([(0, 1)], [(1, 0)]), each((2, 1))])
    z3, m3 = perm("z3", t3), perm("m3", near_b)
    near_a, t4 = mix("t4",
        [near_c, near_x, mid_c, mid_x, both2],
        [[[(0, 0)], [(1, 0)]], [([(2, 0)], [(4, 0)]), ([(3, 0)], [(4, 1)])]],
    )
    z4, m4 = perm("z4", t4), perm("m4", near_a)
    total = add_rows("w2", other(z, 0, 1, 2) + other(near, 0), [(other_c0, 0, 1), (other_c, 0, 2), (near_x, 0, 1)], total)
    (t5m,) = mix("t5m", [both1, z3], [each((0, 0), (1, 0))])
    m5 = perm("m5", t5m)
    (y_nf,) = mix("ynf", [z3, near_c, mid_c], [[[(1, 2)]] + either([(2, 1)], [(0, 0)])])
    got_nf = perm("ynf_", y_nf)
    send3, own3, both3 = partials("X3", [near])
    got3 = perm("y3", send3)
    (t5,) = mix("t5", [m3, own1, got12], [either([(0, 0)], [(1, 0), (2, 0)])])
    z5 = perm("z5", t5)
    (t6m,) = mix("t6m", [both2, z4], [each((0, 0), (1, 0))])
    m6 = perm("m6", t6m)
    (t6,) = mix("t6", [m4, own2, got12], [either([(0, 0)], [(1, 0), (2, 2)])])
    z6 = perm("z6", t6)
    (fm_a,) = mix("fma", [z4, mid_c, mid_x], [[([(1, 0)], [(0, 0)]), ([(2, 0)], [(0, 1)])]])
    send4, own4, both4 = partials("X4", [z])
    (t7,) = mix("t7", [both3, m5], [each((0, 0), (1, 0))])
    z7 = perm("z7", t7)
    (t7m,) = mix("t7m", [own1, got12, z5], [each((0, 0), (1, 0), (2, 0))])
    m7 = perm("m7", t7m)
    (fe_b,) = mix("feb", [z5, m3], [either([(1, 0)], [(0, 0)])])
    fe_other_b = perm("yfe", fe_b)
    total = add_rows("w3",
        own(near, 0, 1, 2) + other(near, 2) + other(far_middle, 1, 2) + own(far_middle, 1, 2, 0) + other(far_middle, 0),
        [(near_c, 0, 3), (got_nf, 0, 3), (y_nf, 1, 2), (fm_a, 0, 2)], total,
    )
    t8m, more_cross = mix("t8m", [own2, got12, z6, other_c], [each((0, 0), (1, 2), (2, 0)), [[(3, 0)]]])
    m8 = perm("m8", t8m)
    near_cross = perm("zn", more_cross)
    (fe_a,) = mix("fea", [z6, m4], [either([(1, 0)], [(0, 0)])])
    (t8,) = mix("t8", [own3, got3, m7], [each((0, 0), (1, 0), (2, 0))])
    z8 = perm("z8", t8)
    got4 = perm("y4", send4)
    theirs, ours = mix("ylast", [both4, z7, m6], [[[(0, place), (1, place), (2, place)]] for place in (1, 0)])
    fin = perm("yfin", theirs)
    total = add_rows("w4",
        own(far_end, 1, 2, 0) + other(far_end, 0, 1, 2) + other(near, 1),
        [(fe_b, 0, 2), (fe_a, 0, 2), (fe_other_b, 0, 2), (near_cross, 0, 1)], total,
    )
    (early,) = mix("early", [own4, got4], [each((0, 0), (1, 0))])
    (input_grad,) = mix("final", [ours, fin, early, z8, m8], [[[(0, 0), (1, 0)]] + each((2, 0), (3, 0), (4, 0))])
    return (input_grad, total)


def plain_per_device(context, out_grad, weight):
    all_grads = lax.all_gather(out_grad, "row", axis=0, tiled=True)
    gathered = lax.all_gather(context, "col", axis=1, tiled=True)
    weight_grad = lax.dot_general(
        gathered, all_grads, (((0,), (0,)), ((), ())), preferred_element_type=jnp.float32
    )
    partial_value = lax.dot_general(
        all_grads, weight, (((1,), (1,)), ((), ())), preferred_element_type=jnp.float32
    )
    input_grad = lax.psum_scatter(
        partial_value.astype(jnp.bfloat16), "col", scatter_dimension=1, tiled=True
    )
    return (input_grad, weight_grad.astype(jnp.bfloat16))


def solution(mesh):
    placed = (P("groups", ("row", "col")), P(("groups", "row"), "col"), P("row", "col"))
    on_grid = mesh.shape["col"] == 8 and mesh.shape["row"] == 2
    return jax.shard_map(
        grid_per_device if on_grid else plain_per_device,
        mesh=mesh,
        in_specs=placed,
        out_specs=(P("groups", ("row", "col")), P(("groups", "row"), "col")),
        check_vma=False,
    )
```
